32 devices in a mesh: groups: 2 (over y), blk: 4 (over z), red: 2 (over x), sub: 2 (over core).
Axes of the slice: x: 2, y: 2, z: 4, core: 2. Of those that a mesh axis runs over, the one named last changes fastest.
Arguments:
- activations: bfloat16 [2, 16, 128, 8192], P('red', ('groups', 'blk', 'sub')), parts along dimension 1, may hold values from -6 to 6
- out_grads: bfloat16 [2, 16, 128, 8192], P('red', ('groups', 'blk', 'sub')), parts along dimension 1, may hold values from -6 to 6
- lengths: int32 [2, 16], P('red', ('groups', 'blk', 'sub')), parts along dimension 1, may hold values from 32 to 128
- proj_in: bfloat16 [8192, 256], P(('blk', 'red', 'sub')), may hold values from -0.0625 to 0.0625
- proj_out: bfloat16 [8192, 256], P(('blk', 'red', 'sub')), may hold values from -0.0625 to 0.0625
- queries: bfloat16 [512, 256, 256], P(('groups', 'red'), ('blk', 'sub')), parts along dimension 0, may hold values from -6 to 6
Outputs:
- scores: float32 [512, 16], P(('groups', 'blk', 'sub'), 'red'), parts along dimension 0
The draws below stay inside these ranges and needn't reach their ends.
There are 2 independent parts, one for each index of `groups`. The reference program is written for one: setup_inputs(seed, part) draws one part's arguments, and reference() takes and returns one part's arrays. A program takes and returns all parts, laid end to end along the dimension named above; an argument that names none is the same for every part. Nothing has to cross between parts.
All inputs are finite; a program needn't handle non-finite values.
Results may differ from the reference program's by a relative error of at most 0.0051.
Values may be sent and summed in bfloat16 or wider, within the bound.
A program may use at most 128 MiB of HBM per device.

```python
import math
import jax
import jax.numpy as jnp
from jax import lax

D = 8192
R = 256
BS = 512
LEN = 128
Q = 256
NS_STEPS = 2
BLOCKS = 128
GROUP_EX = 8
EXAMPLES = 16
N_RED = 2


def set_ends(array, own_key, low, high):
    index_at = [jax.random.randint(jax.random.fold_in(own_key, axis), (), 0, length) for axis, length in enumerate(array.shape)]
    widest = array.shape.index(max(array.shape))
    next_to = index_at[:widest] + [(index_at[widest] + 1) % array.shape[widest]] + index_at[widest + 1:]
    return array.at[tuple(index_at)].set(low).at[tuple(next_to)].set(high)


def steps_of(own_key, dims, cuts, least, top_value):
    def one(position, parts):
        heights = jax.random.uniform(jax.random.fold_in(jax.random.fold_in(own_key, 6), position), (parts,), jnp.float32, least / len(cuts), top_value / len(cuts))
        return jnp.repeat(jnp.exp(heights), dims[position] // parts).reshape((-1,) + (1,) * (len(dims) - position - 1))

    level = one(*cuts[0])
    for cut in cuts[1:]:
        level = level * one(*cut)
    return level


def gaussian(rng, shape, deviation, reach, cuts=(), kind=jnp.bfloat16):
    values = deviation * jax.random.normal(rng, shape, jnp.float32)
    if cuts:
        values = values * steps_of(rng, shape, cuts, -0.22, 0.18)
    return jnp.clip(values, -reach, reach).astype(kind)


def setup_inputs(seed: int = 0, part: int = 0) -> dict:
    key_of = jax.random.split(jax.random.key(seed), 7)
    own_keys = jax.random.split(jax.random.fold_in(key_of[6], part), 7)
    return {
        "activations": gaussian(own_keys[0], (N_RED, GROUP_EX, LEN, D), 1.0, 6.0, ((0, 2), (1, 8))),
        "out_grads": gaussian(own_keys[1], (N_RED, GROUP_EX, LEN, D), 1.0, 6.0, ((0, 2), (1, 8))),
        "lengths": set_ends(jax.random.randint(own_keys[2], (N_RED, GROUP_EX), LEN // 4, LEN + 1), jax.random.fold_in(own_keys[2], 1), LEN // 4, LEN).astype(jnp.int32),
        "proj_in": gaussian(key_of[3], (D, R), D ** -0.5, 0.0625, ((0, 16),)),
        "proj_out": gaussian(key_of[4], (D, R), D ** -0.5, 0.0625, ((0, 16),)),
        "queries": gaussian(own_keys[5], (Q, R, R), 1.0, 6.0, ((0, 2), (1, 8))),
    }


DAMPING = 0.1
HIGH = lax.Precision.HIGHEST

def reference(activations, out_grads, lengths, proj_in, proj_out, queries):
    tokens_all = activations.reshape(EXAMPLES, LEN, D)
    grads_all = out_grads.reshape(EXAMPLES, LEN, D)
    length_all = lengths.reshape(EXAMPLES)

    def project(item):
        tokens_one, grads_one, length_one = item
        live_mask = jnp.arange(LEN, dtype=jnp.int32)[:, None] < length_one
        masked = jnp.where(live_mask, grads_one, jnp.zeros((), grads_one.dtype))
        in_side = jnp.dot(tokens_one, proj_in, preferred_element_type=jnp.float32).astype(jnp.bfloat16)
        out_side = jnp.dot(masked, proj_out, preferred_element_type=jnp.float32).astype(jnp.bfloat16)
        return jnp.dot(out_side.T, in_side, preferred_element_type=jnp.float32).astype(jnp.bfloat16)
    projected = lax.map(project, (tokens_all, grads_all, length_all))
    coords = projected.reshape(EXAMPLES, BLOCKS, BS).astype(jnp.float32)
    fisher = jnp.einsum('ekc,ekd->kcd', coords, coords, precision=HIGH) / EXAMPLES
    ident = jnp.eye(BS, dtype=jnp.float32)
    trace = lax.optimization_barrier(jnp.sum(fisher * ident, axis=(1, 2)))
    damping = DAMPING * trace / BS
    hessian = fisher + damping[:, None, None] * ident
    scale = lax.rsqrt(lax.optimization_barrier(jnp.sum(hessian * hessian, axis=(1, 2))))[:, None, None]
    inverse = scale * (2.0 * ident - scale * hessian)
    for sweep in range(NS_STEPS):
        image = jnp.einsum('kab,kbc->kac', hessian, inverse, precision=HIGH)
        inverse = jnp.einsum('kab,kbc->kac', inverse, 2.0 * ident - image, precision=HIGH)
    query_coords = queries.reshape(Q, BLOCKS, BS).astype(jnp.float32)
    weighted = jnp.einsum('kcd,qkd->kcq', inverse, query_coords, precision=HIGH)
    scores = jnp.einsum('kcq,ekc->qe', weighted, coords, precision=HIGH)
    return scores * (1.0 / math.sqrt(BLOCKS))
```

```python
import math

import jax
import jax.numpy as jnp
from jax import lax
from jax.sharding import PartitionSpec as P

BS = 512
NS_STEPS = 2
BLOCKS = 128


DAMPING = 0.1
HIGH = lax.Precision.HIGHEST


def block_inverse(gram, member, held_blocks):
    size = gram.shape[0]
    ident = jnp.eye(size, dtype=jnp.float32)
    trace = jnp.sum(gram * ident, axis=1, keepdims=True)
    square = jnp.sum(gram * gram, axis=1, keepdims=True)
    trace = jnp.sum(jnp.where(member, trace, 0.0), axis=0, keepdims=True)
    square = jnp.sum(jnp.where(member, square, 0.0), axis=0, keepdims=True)
    damping = DAMPING * trace / BS
    hessian = gram + damping * ident
    scale = lax.rsqrt(square + 2.0 * damping * trace + BS * damping * damping)
    inverse = scale * (2.0 * ident - scale * hessian)
    for sweep in range(NS_STEPS):
        image = jnp.dot(hessian, inverse, precision=HIGH)
        inverse = jnp.dot(inverse, 2.0 * ident - image, precision=HIGH)
    return inverse


def on_device(activations, out_grads, lengths, proj_in, proj_out, queries):
    ex_dev = activations.shape[1]
    seq_len = activations.shape[2]
    model_width = activations.shape[3]
    rank_in = proj_in.shape[1]
    rank_out = proj_out.shape[1]
    positions = lax.broadcasted_iota(jnp.int32, (ex_dev, seq_len), 1)
    live_mask = positions < lengths
    tok_rows = activations.reshape(ex_dev * seq_len, model_width)
    masked = jnp.where(
        live_mask.reshape(ex_dev * seq_len, 1),
        out_grads.reshape(ex_dev * seq_len, model_width),
        jnp.zeros((), out_grads.dtype),
    )
    first_sum = jnp.dot(
        tok_rows,
        lax.all_gather(proj_in, ("blk", "red", "sub"), axis=0, tiled=True),
        preferred_element_type=jnp.float32,
    )
    second_sum = jnp.dot(
        masked,
        lax.all_gather(proj_out, ("blk", "red", "sub"), axis=0, tiled=True),
        preferred_element_type=jnp.float32,
    )
    in_side = first_sum
    out_side = second_sum
    in_side = in_side.astype(jnp.bfloat16).reshape(ex_dev, seq_len, rank_in)
    out_side = out_side.astype(jnp.bfloat16).reshape(ex_dev, seq_len, rank_out)
    projected = jnp.einsum(
        "elo,eli->eoi", out_side, in_side, preferred_element_type=jnp.float32
    ).astype(jnp.bfloat16)
    regrouped = lax.all_to_all(projected, ("blk", "sub"), split_axis=1, concat_axis=0, tiled=True)
    held = regrouped.shape[0]
    coords = regrouped.reshape(held, -1, BS)
    every_coord = lax.all_gather(coords, "red", axis=0, tiled=True)
    total_ex, held_blocks = every_coord.shape[:2]
    by_block = every_coord.transpose(1, 0, 2)
    rows = by_block.reshape(held_blocks * total_ex, BS)
    own = jnp.arange(held_blocks * total_ex) // total_ex
    member = own[:, None] == own[None, :]
    gram = jnp.dot(rows, rows.T, preferred_element_type=jnp.float32)
    gram = jnp.where(member, gram, 0.0) / total_ex
    inverse = block_inverse(gram, member, held_blocks)
    query_coords = queries.reshape(queries.shape[0], -1, BS)
    raw = jnp.einsum("qkd,ked->qke", query_coords, by_block, preferred_element_type=jnp.float32)
    raw = raw.reshape(raw.shape[0], -1)
    fold = jnp.sum(inverse.reshape(-1, held_blocks, total_ex), axis=1)
    partial_scores = jnp.dot(raw, fold, precision=HIGH)
    every_score = lax.all_gather(partial_scores, "red", axis=0, tiled=True)
    scores = lax.psum_scatter(every_score, ("blk", "sub"), scatter_dimension=0, tiled=True)
    here = lax.axis_index("red") * held
    scores = lax.dynamic_slice_in_dim(scores, here, held, axis=1)
    return scores * (1.0 / math.sqrt(BLOCKS))


def solution(mesh):
    placed = (
        P("red", ("groups", "blk", "sub"), None, None),
        P("red", ("groups", "blk", "sub"), None, None),
        P("red", ("groups", "blk", "sub")),
        P(("blk", "red", "sub"), None),
        P(("blk", "red", "sub"), None),
        P(("groups", "red"), ("blk", "sub"), None),
    )
    return jax.shard_map(
        on_device,
        mesh=mesh,
        in_specs=placed,
        out_specs=P(("groups", "blk", "sub"), "red"),
        check_vma=False,
    )
```

```python
import functools
import math

import jax
import jax.numpy as jnp
from jax import lax
from jax.experimental import pallas as pl
from jax.experimental.pallas import tpu as pltpu
from jax.sharding import PartitionSpec as P

BS = 512
NS_STEPS = 2
BLOCKS = 128


DAMPING = 0.1
HIGH = lax.Precision.HIGHEST


def block_inverse(gram, member, held_blocks):
    size = gram.shape[0]
    ident = jnp.eye(size, dtype=jnp.float32)
    trace = jnp.sum(gram * ident, axis=1, keepdims=True)
    square = jnp.sum(gram * gram, axis=1, keepdims=True)
    trace = jnp.sum(jnp.where(member, trace, 0.0), axis=0, keepdims=True)
    square = jnp.sum(jnp.where(member, square, 0.0), axis=0, keepdims=True)
    damping = DAMPING * trace / BS
    hessian = gram + damping * ident
    scale = lax.rsqrt(square + 2.0 * damping * trace + BS * damping * damping)
    inverse = scale * (2.0 * ident - scale * hessian)
    for sweep in range(NS_STEPS):
        image = jnp.dot(hessian, inverse, precision=HIGH)
        inverse = jnp.dot(inverse, 2.0 * ident - image, precision=HIGH)
    return inverse


def on_device(activations, out_grads, lengths, proj_in, proj_out, queries):
    ex_dev = activations.shape[1]
    seq_len = activations.shape[2]
    model_width = activations.shape[3]
    rank_in = proj_in.shape[1]
    rank_out = proj_out.shape[1]
    positions = lax.broadcasted_iota(jnp.int32, (ex_dev, seq_len), 1)
    live_mask = positions < lengths
    tok_rows = activations.reshape(ex_dev * seq_len, model_width)
    masked = jnp.where(
        live_mask.reshape(ex_dev * seq_len, 1),
        out_grads.reshape(ex_dev * seq_len, model_width),
        jnp.zeros((), out_grads.dtype),
    )
    first_sum = jnp.dot(
        tok_rows,
        lax.all_gather(proj_in, ("blk", "red", "sub"), axis=0, tiled=True),
        preferred_element_type=jnp.float32,
    )
    second_sum = jnp.dot(
        masked,
        lax.all_gather(proj_out, ("blk", "red", "sub"), axis=0, tiled=True),
        preferred_element_type=jnp.float32,
    )
    in_side = first_sum
    out_side = second_sum
    in_side = in_side.astype(jnp.bfloat16).reshape(ex_dev, seq_len, rank_in)
    out_side = out_side.astype(jnp.bfloat16).reshape(ex_dev, seq_len, rank_out)
    projected = jnp.einsum(
        "elo,eli->eoi", out_side, in_side, preferred_element_type=jnp.float32
    ).astype(jnp.bfloat16)
    regrouped = lax.all_to_all(projected, ("blk", "sub"), split_axis=1, concat_axis=0, tiled=True)
    held = regrouped.shape[0]
    coords = regrouped.reshape(held, -1, BS)
    every_coord = lax.all_gather(coords, "red", axis=0, tiled=True)
    total_ex, held_blocks = every_coord.shape[:2]
    by_block = every_coord.transpose(1, 0, 2)
    rows = by_block.reshape(held_blocks * total_ex, BS)
    own = jnp.arange(held_blocks * total_ex) // total_ex
    member = own[:, None] == own[None, :]
    gram = jnp.dot(rows, rows.T, preferred_element_type=jnp.float32)
    gram = jnp.where(member, gram, 0.0) / total_ex
    inverse = block_inverse(gram, member, held_blocks)
    query_coords = queries.reshape(queries.shape[0], -1, BS)
    raw = jnp.einsum("qkd,ked->qke", query_coords, by_block, preferred_element_type=jnp.float32)
    raw = raw.reshape(raw.shape[0], -1)
    fold = jnp.sum(inverse.reshape(-1, held_blocks, total_ex), axis=1)
    partial_scores = jnp.dot(raw, fold, precision=HIGH)
    every_score = lax.all_gather(partial_scores, "red", axis=0, tiled=True)
    scores = lax.psum_scatter(every_score, ("blk", "sub"), scatter_dimension=0, tiled=True)
    here = lax.axis_index("red") * held
    scores = lax.dynamic_slice_in_dim(scores, here, held, axis=1)
    return scores * (1.0 / math.sqrt(BLOCKS))


UP, DOWN, ACROSS, OVER, CORE = range(5)


def fused(nz, split, a_hbm, g_hbm, len_ref, pin_hbm, pout_hbm, q_hbm, out_ref, pbuf, abuf, gbuf, qbuf, qt, acc,
          pieces, coords, parts, rbuf, lsem, ssem, rsem, asem_s, asem_r, xsem_s, xsem_r, fsem_s, fsem_r):
    y, z, x, c = (lax.axis_index(name) for name in ("groups", "blk", "red", "sub"))
    rows, rank = pbuf.shape[2:]
    n_tok = abuf.shape[0]
    n_chunk = nz * 2
    me = z * 2 + c

    def slot(zz, xx, cc):
        return (zz * 2 + xx) * 2 + cc

    def remote(src, dst, send, recv, **device):
        return pltpu.make_async_remote_copy(
            src_ref=src, dst_ref=dst, send_sem=send, recv_sem=recv,
            device_id=device, device_id_type=pl.DeviceIdType.MESH)

    own = slot(z, x, c)
    local = [
        pltpu.make_async_copy(pin_hbm, pbuf.at[own, 0], lsem.at[0]),
        pltpu.make_async_copy(pout_hbm, pbuf.at[own, 1], lsem.at[1]),
        pltpu.make_async_copy(q_hbm, qbuf, lsem.at[2]),
        pltpu.make_async_copy(a_hbm, abuf, lsem.at[3]),
        pltpu.make_async_copy(g_hbm, gbuf, lsem.at[4]),
    ]
    for item in local:
        item.start()

    barrier = pltpu.get_barrier_semaphore()
    greeted = 0
    for dx in range(2):
        for step in range(n_chunk):
            if dx == 0 and step == 0:
                continue
            other = lax.rem(me + step, n_chunk)
            pl.semaphore_signal(barrier, inc=1, device_id={"blk": other // 2, "red": lax.rem(x + dx, 2), "sub": lax.rem(other, 2)},
                                device_id_type=pl.DeviceIdType.MESH)
            greeted += 1
    pl.semaphore_signal(barrier, inc=1, device_id={"groups": 1 - y}, device_id_type=pl.DeviceIdType.MESH)
    pl.semaphore_wait(barrier, greeted + 1)

    pending = []

    def part(p, at):
        if isinstance(p, int):
            return pbuf.at[at, :, pl.ds(split, rows - split), :]
        return pbuf.at[at, p, pl.ds(0, split), :]

    targets = {UP: lambda: {"blk": lax.min(z + 1, nz - 1)}, DOWN: lambda: {"blk": lax.max(z - 1, 0)},
               ACROSS: lambda: {"red": 1 - x}, OVER: lambda: {"groups": 1 - y}, CORE: lambda: {"sub": 1 - c}}

    def moved(way, p, at):
        return remote(part(p, at), part(p, at), ssem.at[way, p, at], rsem.at[p, at], **targets[way]())

    def send(way, p, at, when=None):
        if when is None:
            moved(way, p, at).start()
        else:
            pl.when(when)(lambda: moved(way, p, at).start())
        pending.append((way, p, at, when))

    def arrived(p, at):
        moved(CORE, p, at).wait_recv()

    def multiply(at, first=False):
        columns = pl.ds(pl.multiple_of(at * rows, rows), rows)
        for side, tokens in enumerate((abuf, gbuf)):
            term = jnp.dot(tokens[:, columns], pbuf[at, side], preferred_element_type=jnp.float32)
            acc[side] = term if first else acc[side] + term

    turns = [sorted(range(nz), key=lambda other: (abs(other - here), other)) for here in range(nz)]

    def turn(k):
        return sum(jnp.where(z == here, turns[here][k], 0) for here in range(nz)).astype(jnp.int32)

    local[0].wait()
    local[1].wait()
    for p in (y, 2):
        send(UP, p, own, z < nz - 1)
        send(DOWN, p, own, z > 0)
        send(ACROSS, p, own)
    for p in (y, 1 - y, 2):
        send(CORE, p, own)

    local[2].wait()
    hh, kb = qt.shape[0], qt.shape[1]
    step_q = 16

    def regroup(i, carry):
        at = pl.ds(pl.multiple_of(i * step_q, step_q), step_q)
        block = jnp.swapaxes(qbuf[at].astype(jnp.float32), 0, 1).astype(jnp.bfloat16)
        block = block.reshape(kb, hh, step_q, rank)
        for h in range(hh):
            qt[h, :, at, :] = block[:, h]
        return carry

    lax.fori_loop(0, qbuf.shape[0] // step_q, regroup, 0)
    local[3].wait()
    local[4].wait()
    multiply(own, True)

    waiting, twin = [], [slot(z, x, 1 - c)]
    for k in range(1, nz + 2):
        fresh = []
        if k < nz:
            zk = turn(k)
            at = slot(zk, x, c)
            for p in (y, 2):
                arrived(p, at)
                send(UP, p, at, jnp.logical_and(zk < z, z < nz - 1))
                send(DOWN, p, at, jnp.logical_and(zk > z, z > 0))
                send(ACROSS, p, at)
                if not isinstance(p, int):
                    send(OVER, p, at)
                send(CORE, p, at)
            fresh.append((zk, x))
        if k <= nz:
            zk = turn(k - 1)
            at = slot(zk, 1 - x, c)
            for p in (y, 2):
                arrived(p, at)
                if not isinstance(p, int):
                    send(OVER, p, at)
                send(CORE, p, at)
            fresh.append((zk, 1 - x))
        for zk, xk in waiting:
            at = slot(zk, xk, c)
            arrived(1 - y, at)
            send(CORE, 1 - y, at)
        for at in twin:
            for p in (y, 1 - y, 2):
                arrived(p, at)
            multiply(at)
        for zk, xk in waiting:
            multiply(slot(zk, xk, c))
        twin = [slot(zk, xk, 1 - c) for zk, xk in waiting]
        waiting = fresh
    for at in twin:
        for p in (y, 1 - y, 2):
            arrived(p, at)
        multiply(at)

    chunk_rows = hh * kb
    old = lax.broadcasted_iota(jnp.int32, (rank, rank), 0)
    new = lax.broadcasted_iota(jnp.int32, (rank, rank), 1)
    inside = jnp.bitwise_and(new, chunk_rows - 1)
    source = new - inside + jnp.bitwise_and(inside, kb - 1) * hh + lax.shift_right_logical(inside, kb.bit_length() - 1)
    order = jnp.where(old == source, 1.0, 0.0).astype(jnp.bfloat16)
    in_side = acc[0].astype(jnp.bfloat16)
    live = lax.broadcasted_iota(jnp.int32, (n_tok, rank), 0) < len_ref[0, 0]
    out_side = jnp.where(live, acc[1], 0.0).astype(jnp.bfloat16)
    out_side = jnp.dot(out_side, order, preferred_element_type=jnp.float32).astype(jnp.bfloat16)
    projected = lax.dot_general(out_side, in_side, (((0,), (0,)), ((), ())), preferred_element_type=jnp.float32)
    pieces[...] = projected.astype(jnp.bfloat16).reshape(pieces.shape)

    def chunk_out(to):
        return remote(pieces.at[to], coords.at[x * n_chunk + me], asem_s.at[to], asem_r.at[me], blk=to // 2, sub=lax.rem(to, 2))

    def chunk_in(frm):
        return remote(pieces.at[frm], coords.at[x * n_chunk + frm], asem_s.at[frm], asem_r.at[frm], sub=1 - c)

    def across(of, side):
        return remote(coords.at[side * n_chunk + of], coords.at[side * n_chunk + of], xsem_s.at[of], xsem_r.at[of], red=1 - x)

    for step in range(1, n_chunk):
        chunk_out(lax.rem(me + step, n_chunk)).start()
    coords[x * n_chunk + me] = pieces[me]
    across(me, x).start()
    for step in [1, 7, 2, 6, 3, 5, 4] if n_chunk == 8 else range(1, n_chunk):
        frm = lax.rem(me + step, n_chunk)
        chunk_in(frm).wait_recv()
        across(frm, x).start()
    for of in range(n_chunk):
        across(of, 1 - x).wait_recv()

    n_ex = coords.shape[0]
    size = n_ex * kb
    halves = [coords[:, h].reshape(size, rank) for h in range(hh)]
    row = lax.broadcasted_iota(jnp.int32, (size, size), 0)
    col = lax.broadcasted_iota(jnp.int32, (size, size), 1)
    member = jnp.bitwise_and(row, kb - 1) == jnp.bitwise_and(col, kb - 1)
    contract = (((1,), (1,)), ((), ()))
    gram = sum(lax.dot_general(half, half, contract, preferred_element_type=jnp.float32) for half in halves)
    gram = jnp.where(member, gram, 0.0) / n_ex
    ident = jnp.where(row == col, 1.0, 0.0)
    trace = jnp.sum(gram * ident, axis=1, keepdims=True)
    square = jnp.sum(gram * gram, axis=1, keepdims=True)
    trace = jnp.sum(jnp.where(member, trace, 0.0), axis=0, keepdims=True)
    square = jnp.sum(jnp.where(member, square, 0.0), axis=0, keepdims=True)
    damping = DAMPING * trace / BS
    hessian = gram + damping * ident
    scale = lax.rsqrt(square + 2.0 * damping * trace + BS * damping * damping)
    inverse = scale * (2.0 * ident - scale * hessian)

    n_q = qt.shape[2]
    lane = jnp.bitwise_and(lax.broadcasted_iota(jnp.int32, (n_q, size), 1), kb - 1)
    flipped = [half.T for half in halves]
    raw = jnp.zeros((n_q, size), jnp.float32)
    for k in range(kb):
        term = sum(jnp.dot(qt[h, k], flipped[h], preferred_element_type=jnp.float32) for h in range(hh))
        raw = jnp.where(lane == k, term, raw)

    for sweep in range(NS_STEPS):
        image = jnp.dot(hessian, inverse, precision=HIGH, preferred_element_type=jnp.float32)
        rest = 2.0 * ident - image
        if sweep < NS_STEPS - 1:
            inverse = jnp.dot(inverse, rest, precision=HIGH, preferred_element_type=jnp.float32)
    raw = jnp.dot(raw, inverse, precision=HIGH, preferred_element_type=jnp.float32)
    raw = jnp.dot(raw, rest, precision=HIGH, preferred_element_type=jnp.float32)
    ex = lax.broadcasted_iota(jnp.int32, (n_ex, size), 0)
    of_ex = lax.shift_right_logical(lax.broadcasted_iota(jnp.int32, (n_ex, size), 1), kb.bit_length() - 1)
    fold = jnp.where(ex == of_ex, 1.0, 0.0)
    total = lax.dot_general(fold, raw, contract, precision=HIGH, preferred_element_type=jnp.float32)
    parts[...] = total.reshape(parts.shape)

    takers = n_chunk // 2

    def score_out(xx, t):
        to = takers * x + t
        return remote(parts.at[xx], rbuf.at[me], fsem_s.at[xx * takers + t], fsem_r.at[me],
                      blk=to // 2, red=jnp.int32(xx), sub=lax.rem(to, 2))

    def is_self(xx, t):
        return jnp.logical_and(takers * x + t == me, x == xx)

    for xx in range(2):
        for t in range(takers):
            pl.when(jnp.logical_not(is_self(xx, t)))(lambda: score_out(xx, t).start())
    giver = me // takers

    @pl.when(giver == x)
    def _():
        rbuf[me] = parts[x]

    for frm in range(n_chunk):
        landing = remote(parts.at[0], rbuf.at[frm], fsem_s.at[0], fsem_r.at[frm], sub=1 - c)
        pl.when(jnp.logical_not(jnp.logical_and(giver == x, me == frm)))(landing.wait_recv)
    out_ref[...] = jnp.sum(rbuf[...], axis=0)

    for xx in range(2):
        for t in range(takers):
            pl.when(jnp.logical_not(is_self(xx, t)))(lambda: score_out(xx, t).wait_send())
    for step in range(1, n_chunk):
        chunk_out(lax.rem(me + step, n_chunk)).wait_send()
    for of in range(n_chunk):
        across(of, x).wait_send()
    for way, p, at, when in pending:
        if when is None:
            moved(way, p, at).wait_send()
        else:
            pl.when(when)(lambda: moved(way, p, at).wait_send())


def on_device_fused(activations, out_grads, lengths, proj_in, proj_out, queries):
    nz = lax.axis_size("blk")
    seq_len, width = activations.shape[2:]
    rows, rank = proj_in.shape
    n_q, held_rows, _ = queries.shape
    hh = BS // rank
    kb = held_rows // hh
    n_chunk = nz * 2
    n_ex = n_chunk * 2
    split = rows * 11 // 16
    anywhere = pl.BlockSpec(memory_space=pl.ANY)
    dma = pltpu.SemaphoreType.DMA
    flops = 4 * seq_len * width * rank
    total = pl.pallas_call(
        functools.partial(fused, nz, split),
        out_shape=jax.ShapeDtypeStruct((n_chunk, n_q), jnp.float32),
        in_specs=[anywhere, anywhere, pl.BlockSpec(memory_space=pltpu.SMEM), anywhere, anywhere, anywhere],
        out_specs=pl.BlockSpec(memory_space=pltpu.VMEM),
        scratch_shapes=[
            pltpu.VMEM((n_chunk * 2, 2, rows, rank), jnp.bfloat16),
            pltpu.VMEM((seq_len, width), jnp.bfloat16),
            pltpu.VMEM((seq_len, width), jnp.bfloat16),
            pltpu.VMEM(queries.shape, jnp.bfloat16),
            pltpu.VMEM((hh, kb, n_q, rank), jnp.bfloat16),
            pltpu.VMEM((2, seq_len, rank), jnp.float32),
            pltpu.VMEM((n_chunk, hh, kb, rank), jnp.bfloat16),
            pltpu.VMEM((n_ex, hh, kb, rank), jnp.bfloat16),
            pltpu.VMEM((2, n_chunk, n_q), jnp.float32),
            pltpu.VMEM((n_chunk, n_chunk, n_q), jnp.float32),
            dma((5,)),
            dma((5, 3, n_chunk * 2)),
            dma((3, n_chunk * 2)),
            dma((n_chunk,)),
            dma((n_chunk,)),
            dma((n_chunk,)),
            dma((n_chunk,)),
            dma((n_chunk,)),
            dma((n_chunk,)),
        ],
        compiler_params=pltpu.CompilerParams(collective_id=0, has_side_effects=True, vmem_limit_bytes=48 * 2**20),
        cost_estimate=pl.CostEstimate(flops=flops, bytes_accessed=7 * 2**20, transcendentals=0),
    )(activations.reshape(seq_len, width), out_grads.reshape(seq_len, width), lengths, proj_in, proj_out, queries)
    n_out = n_q * 2 // n_chunk
    me = lax.axis_index("blk") * 2 + lax.axis_index("sub")
    mine = lax.dynamic_slice_in_dim(total, lax.rem(me, n_chunk // 2) * n_out, n_out, axis=1)
    return mine.T * (1.0 / math.sqrt(BLOCKS))


def fits(mesh):
    shape = mesh.shape
    return shape["groups"] == 2 and shape["red"] == 2 and shape["sub"] == 2 and shape["blk"] == 4


def solution(mesh):
    placed = (
        P("red", ("groups", "blk", "sub"), None, None),
        P("red", ("groups", "blk", "sub"), None, None),
        P("red", ("groups", "blk", "sub")),
        P(("blk", "red", "sub"), None),
        P(("blk", "red", "sub"), None),
        P(("groups", "red"), ("blk", "sub"), None),
    )
    return jax.shard_map(
        on_device_fused if fits(mesh) else on_device,
        mesh=mesh,
        in_specs=placed,
        out_specs=P(("groups", "blk", "sub"), "red"),
        check_vma=False,
    )
```

```python
import functools
import math

import jax
import jax.numpy as jnp
from jax import lax
from jax.experimental import pallas as pl
from jax.experimental.pallas import tpu as pltpu
from jax.sharding import PartitionSpec as P

BS = 512
NS_STEPS = 2
BLOCKS = 128


DAMPING = 0.1
HIGH = lax.Precision.HIGHEST


def block_inverse(gram, member, held_blocks):
    size = gram.shape[0]
    ident = jnp.eye(size, dtype=jnp.float32)
    trace = jnp.sum(gram * ident, axis=1, keepdims=True)
    square = jnp.sum(gram * gram, axis=1, keepdims=True)
    trace = jnp.sum(jnp.where(member, trace, 0.0), axis=0, keepdims=True)
    square = jnp.sum(jnp.where(member, square, 0.0), axis=0, keepdims=True)
    damping = DAMPING * trace / BS
    hessian = gram + damping * ident
    scale = lax.rsqrt(square + 2.0 * damping * trace + BS * damping * damping)
    inverse = scale * (2.0 * ident - scale * hessian)
    for sweep in range(NS_STEPS):
        image = jnp.dot(hessian, inverse, precision=HIGH)
        inverse = jnp.dot(inverse, 2.0 * ident - image, precision=HIGH)
    return inverse


def on_device(activations, out_grads, lengths, proj_in, proj_out, queries):
    ex_dev = activations.shape[1]
    seq_len = activations.shape[2]
    model_width = activations.shape[3]
    rank_in = proj_in.shape[1]
    rank_out = proj_out.shape[1]
    positions = lax.broadcasted_iota(jnp.int32, (ex_dev, seq_len), 1)
    live_mask = positions < lengths
    tok_rows = activations.reshape(ex_dev * seq_len, model_width)
    masked = jnp.where(
        live_mask.reshape(ex_dev * seq_len, 1),
        out_grads.reshape(ex_dev * seq_len, model_width),
        jnp.zeros((), out_grads.dtype),
    )
    first_sum = jnp.dot(
        tok_rows,
        lax.all_gather(proj_in, ("blk", "red", "sub"), axis=0, tiled=True),
        preferred_element_type=jnp.float32,
    )
    second_sum = jnp.dot(
        masked,
        lax.all_gather(proj_out, ("blk", "red", "sub"), axis=0, tiled=True),
        preferred_element_type=jnp.float32,
    )
    in_side = first_sum
    out_side = second_sum
    in_side = in_side.astype(jnp.bfloat16).reshape(ex_dev, seq_len, rank_in)
    out_side = out_side.astype(jnp.bfloat16).reshape(ex_dev, seq_len, rank_out)
    projected = jnp.einsum(
        "elo,eli->eoi", out_side, in_side, preferred_element_type=jnp.float32
    ).astype(jnp.bfloat16)
    regrouped = lax.all_to_all(projected, ("blk", "sub"), split_axis=1, concat_axis=0, tiled=True)
    held = regrouped.shape[0]
    coords = regrouped.reshape(held, -1, BS)
    every_coord = lax.all_gather(coords, "red", axis=0, tiled=True)
    total_ex, held_blocks = every_coord.shape[:2]
    by_block = every_coord.transpose(1, 0, 2)
    rows = by_block.reshape(held_blocks * total_ex, BS)
    own = jnp.arange(held_blocks * total_ex) // total_ex
    member = own[:, None] == own[None, :]
    gram = jnp.dot(rows, rows.T, preferred_element_type=jnp.float32)
    gram = jnp.where(member, gram, 0.0) / total_ex
    inverse = block_inverse(gram, member, held_blocks)
    query_coords = queries.reshape(queries.shape[0], -1, BS)
    raw = jnp.einsum("qkd,ked->qke", query_coords, by_block, preferred_element_type=jnp.float32)
    raw = raw.reshape(raw.shape[0], -1)
    fold = jnp.sum(inverse.reshape(-1, held_blocks, total_ex), axis=1)
    partial_scores = jnp.dot(raw, fold, precision=HIGH)
    every_score = lax.all_gather(partial_scores, "red", axis=0, tiled=True)
    scores = lax.psum_scatter(every_score, ("blk", "sub"), scatter_dimension=0, tiled=True)
    here = lax.axis_index("red") * held
    scores = lax.dynamic_slice_in_dim(scores, here, held, axis=1)
    return scores * (1.0 / math.sqrt(BLOCKS))


UP, DOWN, ACROSS, OVER, CORE = range(5)


def fused(nz, split, a_hbm, g_hbm, len_ref, pin_hbm, pout_hbm, q_hbm, out_ref, pbuf, abuf, gbuf, qbuf, qt, acc,
          pieces, coords, parts, rbuf, lsem, ssem, rsem, asem_s, asem_r, xsem_s, xsem_r, fsem_s, fsem_r):
    y, z, x, c = (lax.axis_index(name) for name in ("groups", "blk", "red", "sub"))
    rows, rank = pbuf.shape[2:]
    n_tok = abuf.shape[0]
    n_chunk = nz * 2
    me = z * 2 + c

    def slot(zz, xx, cc):
        return (zz * 2 + xx) * 2 + cc

    def remote(src, dst, send, recv, **device):
        return pltpu.make_async_remote_copy(
            src_ref=src, dst_ref=dst, send_sem=send, recv_sem=recv,
            device_id=device, device_id_type=pl.DeviceIdType.MESH)

    own = slot(z, x, c)
    local = [
        pltpu.make_async_copy(pin_hbm, pbuf.at[own, 0], lsem.at[0]),
        pltpu.make_async_copy(pout_hbm, pbuf.at[own, 1], lsem.at[1]),
        pltpu.make_async_copy(q_hbm, qbuf, lsem.at[2]),
        pltpu.make_async_copy(a_hbm, abuf, lsem.at[3]),
        pltpu.make_async_copy(g_hbm, gbuf, lsem.at[4]),
    ]
    for item in local:
        item.start()

    barrier = pltpu.get_barrier_semaphore()

    def greet(**device):
        pl.semaphore_signal(barrier, inc=1, device_id=device, device_id_type=pl.DeviceIdType.MESH)

    pl.when(z < nz - 1)(lambda: greet(blk=lax.min(z + 1, nz - 1)))
    pl.when(z > 0)(lambda: greet(blk=lax.max(z - 1, 0)))
    greet(red=1 - x)
    greet(groups=1 - y)
    greet(sub=1 - c)
    pl.semaphore_wait(barrier, 3 + (z < nz - 1).astype(jnp.int32) + (z > 0).astype(jnp.int32))

    pending = []

    def part(p, at):
        if isinstance(p, int):
            return pbuf.at[at, :, pl.ds(split, rows - split), :]
        return pbuf.at[at, p, pl.ds(0, split), :]

    targets = {UP: lambda: {"blk": lax.min(z + 1, nz - 1)}, DOWN: lambda: {"blk": lax.max(z - 1, 0)},
               ACROSS: lambda: {"red": 1 - x}, OVER: lambda: {"groups": 1 - y}, CORE: lambda: {"sub": 1 - c}}

    def moved(way, p, at):
        return remote(part(p, at), part(p, at), ssem.at[way, p, at], rsem.at[p, at], **targets[way]())

    def send(way, p, at, when=None):
        if when is None:
            moved(way, p, at).start()
        else:
            pl.when(when)(lambda: moved(way, p, at).start())
        pending.append((way, p, at, when))

    def arrived(p, at):
        moved(CORE, p, at).wait_recv()

    def multiply(at, first=False):
        columns = pl.ds(pl.multiple_of(at * rows, rows), rows)
        for side, tokens in enumerate((abuf, gbuf)):
            term = jnp.dot(tokens[:, columns], pbuf[at, side], preferred_element_type=jnp.float32)
            acc[side] = term if first else acc[side] + term

    turns = [sorted(range(nz), key=lambda other: (abs(other - here), other)) for here in range(nz)]

    def turn(k):
        return sum(jnp.where(z == here, turns[here][k], 0) for here in range(nz)).astype(jnp.int32)

    local[0].wait()
    local[1].wait()
    for p in (y, 2):
        send(UP, p, own, z < nz - 1)
        send(DOWN, p, own, z > 0)
        send(ACROSS, p, own)
    for p in (y, 1 - y, 2):
        send(CORE, p, own)

    local[2].wait()
    hh, kb = qt.shape[0], qt.shape[1]
    step_q = 16

    def regroup(i, carry):
        at = pl.ds(pl.multiple_of(i * step_q, step_q), step_q)
        block = jnp.swapaxes(qbuf[at].astype(jnp.float32), 0, 1).astype(jnp.bfloat16)
        block = block.reshape(kb, hh, step_q, rank)
        for h in range(hh):
            qt[h, :, at, :] = block[:, h]
        return carry

    lax.fori_loop(0, qbuf.shape[0] // step_q, regroup, 0)
    local[3].wait()
    local[4].wait()
    multiply(own, True)

    waiting, twin = [], [slot(z, x, 1 - c)]
    for k in range(1, nz + 2):
        fresh = []
        if k < nz:
            zk = turn(k)
            at = slot(zk, x, c)
            for p in (y, 2):
                arrived(p, at)
                send(UP, p, at, jnp.logical_and(zk < z, z < nz - 1))
                send(DOWN, p, at, jnp.logical_and(zk > z, z > 0))
                send(ACROSS, p, at)
                if not isinstance(p, int):
                    send(OVER, p, at)
                send(CORE, p, at)
            fresh.append((zk, x))
        if k <= nz:
            zk = turn(k - 1)
            at = slot(zk, 1 - x, c)
            for p in (y, 2):
                arrived(p, at)
                if not isinstance(p, int):
                    send(OVER, p, at)
                send(CORE, p, at)
            fresh.append((zk, 1 - x))
        for zk, xk in waiting:
            at = slot(zk, xk, c)
            arrived(1 - y, at)
            send(CORE, 1 - y, at)
        for at in twin:
            for p in (y, 1 - y, 2):
                arrived(p, at)
            multiply(at)
        for zk, xk in waiting:
            multiply(slot(zk, xk, c))
        twin = [slot(zk, xk, 1 - c) for zk, xk in waiting]
        waiting = fresh
    for at in twin:
        for p in (y, 1 - y, 2):
            arrived(p, at)
        multiply(at)

    chunk_rows = hh * kb
    old = lax.broadcasted_iota(jnp.int32, (rank, rank), 0)
    new = lax.broadcasted_iota(jnp.int32, (rank, rank), 1)
    inside = jnp.bitwise_and(new, chunk_rows - 1)
    source = new - inside + jnp.bitwise_and(inside, kb - 1) * hh + lax.shift_right_logical(inside, kb.bit_length() - 1)
    order = jnp.where(old == source, 1.0, 0.0).astype(jnp.bfloat16)
    in_side = acc[0].astype(jnp.bfloat16)
    live = lax.broadcasted_iota(jnp.int32, (n_tok, rank), 0) < len_ref[0, 0]
    out_side = jnp.where(live, acc[1], 0.0).astype(jnp.bfloat16)
    out_side = jnp.dot(out_side, order, preferred_element_type=jnp.float32).astype(jnp.bfloat16)
    projected = lax.dot_general(out_side, in_side, (((0,), (0,)), ((), ())), preferred_element_type=jnp.float32)
    pieces[...] = projected.astype(jnp.bfloat16).reshape(pieces.shape)

    def chunk_out(to):
        return remote(pieces.at[to], coords.at[x * n_chunk + me], asem_s.at[to], asem_r.at[me], blk=to // 2, sub=lax.rem(to, 2))

    def chunk_in(frm):
        return remote(pieces.at[frm], coords.at[x * n_chunk + frm], asem_s.at[frm], asem_r.at[frm], sub=1 - c)

    def across(of, side):
        return remote(coords.at[side * n_chunk + of], coords.at[side * n_chunk + of], xsem_s.at[of], xsem_r.at[of], red=1 - x)

    for step in range(1, n_chunk):
        chunk_out(lax.rem(me + step, n_chunk)).start()
    coords[x * n_chunk + me] = pieces[me]
    across(me, x).start()
    for step in [1, 7, 2, 6, 3, 5, 4] if n_chunk == 8 else range(1, n_chunk):
        frm = lax.rem(me + step, n_chunk)
        chunk_in(frm).wait_recv()
        across(frm, x).start()
    for of in range(n_chunk):
        across(of, 1 - x).wait_recv()

    n_ex = coords.shape[0]
    size = n_ex * kb
    halves = [coords[:, h].reshape(size, rank) for h in range(hh)]
    row = lax.broadcasted_iota(jnp.int32, (size, size), 0)
    col = lax.broadcasted_iota(jnp.int32, (size, size), 1)
    member = jnp.bitwise_and(row, kb - 1) == jnp.bitwise_and(col, kb - 1)
    contract = (((1,), (1,)), ((), ()))
    gram = sum(lax.dot_general(half, half, contract, preferred_element_type=jnp.float32) for half in halves)
    gram = jnp.where(member, gram, 0.0) / n_ex
    ident = jnp.where(row == col, 1.0, 0.0)
    trace = jnp.sum(gram * ident, axis=1, keepdims=True)
    square = jnp.sum(gram * gram, axis=1, keepdims=True)
    trace = jnp.sum(jnp.where(member, trace, 0.0), axis=0, keepdims=True)
    square = jnp.sum(jnp.where(member, square, 0.0), axis=0, keepdims=True)
    damping = DAMPING * trace / BS
    hessian = gram + damping * ident
    scale = lax.rsqrt(square + 2.0 * damping * trace + BS * damping * damping)
    inverse = scale * (2.0 * ident - scale * hessian)

    n_q = qt.shape[2]
    lane = jnp.bitwise_and(lax.broadcasted_iota(jnp.int32, (n_q, size), 1), kb - 1)
    flipped = [half.T for half in halves]
    raw = jnp.zeros((n_q, size), jnp.float32)
    for k in range(kb):
        term = sum(jnp.dot(qt[h, k], flipped[h], preferred_element_type=jnp.float32) for h in range(hh))
        raw = jnp.where(lane == k, term, raw)

    for sweep in range(NS_STEPS):
        image = jnp.dot(hessian, inverse, precision=HIGH, preferred_element_type=jnp.float32)
        rest = 2.0 * ident - image
        if sweep < NS_STEPS - 1:
            inverse = jnp.dot(inverse, rest, precision=HIGH, preferred_element_type=jnp.float32)
    raw = jnp.dot(raw, inverse, precision=HIGH, preferred_element_type=jnp.float32)
    raw = jnp.dot(raw, rest, precision=HIGH, preferred_element_type=jnp.float32)
    ex = lax.broadcasted_iota(jnp.int32, (n_ex, size), 0)
    of_ex = lax.shift_right_logical(lax.broadcasted_iota(jnp.int32, (n_ex, size), 1), kb.bit_length() - 1)
    fold = jnp.where(ex == of_ex, 1.0, 0.0)
    total = lax.dot_general(fold, raw, contract, precision=HIGH, preferred_element_type=jnp.float32)
    parts[...] = total.reshape(parts.shape)

    takers = n_chunk // 2

    def score_out(xx, t):
        to = takers * x + t
        return remote(parts.at[xx], rbuf.at[me], fsem_s.at[xx * takers + t], fsem_r.at[me],
                      blk=to // 2, red=jnp.int32(xx), sub=lax.rem(to, 2))

    def is_self(xx, t):
        return jnp.logical_and(takers * x + t == me, x == xx)

    for xx in range(2):
        for t in range(takers):
            pl.when(jnp.logical_not(is_self(xx, t)))(lambda: score_out(xx, t).start())
    giver = me // takers

    @pl.when(giver == x)
    def _():
        rbuf[me] = parts[x]

    for frm in range(n_chunk):
        landing = remote(parts.at[0], rbuf.at[frm], fsem_s.at[0], fsem_r.at[frm], sub=1 - c)
        pl.when(jnp.logical_not(jnp.logical_and(giver == x, me == frm)))(landing.wait_recv)
    out_ref[...] = jnp.sum(rbuf[...], axis=0)

    for xx in range(2):
        for t in range(takers):
            pl.when(jnp.logical_not(is_self(xx, t)))(lambda: score_out(xx, t).wait_send())
    for step in range(1, n_chunk):
        chunk_out(lax.rem(me + step, n_chunk)).wait_send()
    for of in range(n_chunk):
        across(of, x).wait_send()
    for way, p, at, when in pending:
        if when is None:
            moved(way, p, at).wait_send()
        else:
            pl.when(when)(lambda: moved(way, p, at).wait_send())


def on_device_fused(activations, out_grads, lengths, proj_in, proj_out, queries):
    nz = lax.axis_size("blk")
    seq_len, width = activations.shape[2:]
    rows, rank = proj_in.shape
    n_q, held_rows, _ = queries.shape
    hh = BS // rank
    kb = held_rows // hh
    n_chunk = nz * 2
    n_ex = n_chunk * 2
    split = rows * 10 // 16
    anywhere = pl.BlockSpec(memory_space=pltpu.HBM)
    dma = pltpu.SemaphoreType.DMA
    flops = 4 * seq_len * width * rank
    total = pl.pallas_call(
        functools.partial(fused, nz, split),
        out_shape=jax.ShapeDtypeStruct((n_chunk, n_q), jnp.float32),
        in_specs=[anywhere, anywhere, pl.BlockSpec(memory_space=pltpu.SMEM), anywhere, anywhere, anywhere],
        out_specs=pl.BlockSpec(memory_space=pltpu.VMEM),
        scratch_shapes=[
            pltpu.VMEM((n_chunk * 2, 2, rows, rank), jnp.bfloat16),
            pltpu.VMEM((seq_len, width), jnp.bfloat16),
            pltpu.VMEM((seq_len, width), jnp.bfloat16),
            pltpu.VMEM(queries.shape, jnp.bfloat16),
            pltpu.VMEM((hh, kb, n_q, rank), jnp.bfloat16),
            pltpu.VMEM((2, seq_len, rank), jnp.float32),
            pltpu.VMEM((n_chunk, hh, kb, rank), jnp.bfloat16),
            pltpu.VMEM((n_ex, hh, kb, rank), jnp.bfloat16),
            pltpu.VMEM((2, n_chunk, n_q), jnp.float32),
            pltpu.VMEM((n_chunk, n_chunk, n_q), jnp.float32),
            dma((5,)),
            dma((5, 3, n_chunk * 2)),
            dma((3, n_chunk * 2)),
            dma((n_chunk,)),
            dma((n_chunk,)),
            dma((n_chunk,)),
            dma((n_chunk,)),
            dma((n_chunk,)),
            dma((n_chunk,)),
        ],
        compiler_params=pltpu.CompilerParams(collective_id=0, has_side_effects=True, vmem_limit_bytes=63 * 2**20),
        cost_estimate=pl.CostEstimate(flops=flops, bytes_accessed=7 * 2**20, transcendentals=0),
    )(activations.reshape(seq_len, width), out_grads.reshape(seq_len, width), lengths, proj_in, proj_out, queries)
    n_out = n_q * 2 // n_chunk
    me = lax.axis_index("blk") * 2 + lax.axis_index("sub")
    mine = lax.dynamic_slice_in_dim(total, lax.rem(me, n_chunk // 2) * n_out, n_out, axis=1)
    return mine.T * (1.0 / math.sqrt(BLOCKS))


def fits(mesh):
    shape = mesh.shape
    return shape["groups"] == 2 and shape["red"] == 2 and shape["sub"] == 2 and shape["blk"] == 4


def solution(mesh):
    placed = (
        P("red", ("groups", "blk", "sub"), None, None),
        P("red", ("groups", "blk", "sub"), None, None),
        P("red", ("groups", "blk", "sub")),
        P(("blk", "red", "sub"), None),
        P(("blk", "red", "sub"), None),
        P(("groups", "red"), ("blk", "sub"), None),
    )
    return jax.shard_map(
        on_device_fused if fits(mesh) else on_device,
        mesh=mesh,
        in_specs=placed,
        out_specs=P(("groups", "blk", "sub"), "red"),
        check_vma=False,
    )
```

```python
import functools
import math

import jax
import jax.numpy as jnp
from jax import lax
from jax.experimental import pallas as pl
from jax.experimental.pallas import tpu as pltpu
from jax.sharding import PartitionSpec as P

BS = 512
NS_STEPS = 2
BLOCKS = 128


DAMPING = 0.1
HIGH = lax.Precision.HIGHEST


def block_inverse(gram, member, held_blocks):
    size = gram.shape[0]
    ident = jnp.eye(size, dtype=jnp.float32)
    trace = jnp.sum(gram * ident, axis=1, keepdims=True)
    square = jnp.sum(gram * gram, axis=1, keepdims=True)
    trace = jnp.sum(jnp.where(member, trace, 0.0), axis=0, keepdims=True)
    square = jnp.sum(jnp.where(member, square, 0.0), axis=0, keepdims=True)
    damping = DAMPING * trace / BS
    hessian = gram + damping * ident
    scale = lax.rsqrt(square + 2.0 * damping * trace + BS * damping * damping)
    inverse = scale * (2.0 * ident - scale * hessian)
    for sweep in range(NS_STEPS):
        image = jnp.dot(hessian, inverse, precision=HIGH)
        inverse = jnp.dot(inverse, 2.0 * ident - image, precision=HIGH)
    return inverse


def on_device(activations, out_grads, lengths, proj_in, proj_out, queries):
    ex_dev = activations.shape[1]
    seq_len = activations.shape[2]
    model_width = activations.shape[3]
    rank_in = proj_in.shape[1]
    rank_out = proj_out.shape[1]
    positions = lax.broadcasted_iota(jnp.int32, (ex_dev, seq_len), 1)
    live_mask = positions < lengths
    tok_rows = activations.reshape(ex_dev * seq_len, model_width)
    masked = jnp.where(
        live_mask.reshape(ex_dev * seq_len, 1),
        out_grads.reshape(ex_dev * seq_len, model_width),
        jnp.zeros((), out_grads.dtype),
    )
    first_sum = jnp.dot(
        tok_rows,
        lax.all_gather(proj_in, ("blk", "red", "sub"), axis=0, tiled=True),
        preferred_element_type=jnp.float32,
    )
    second_sum = jnp.dot(
        masked,
        lax.all_gather(proj_out, ("blk", "red", "sub"), axis=0, tiled=True),
        preferred_element_type=jnp.float32,
    )
    in_side = first_sum
    out_side = second_sum
    in_side = in_side.astype(jnp.bfloat16).reshape(ex_dev, seq_len, rank_in)
    out_side = out_side.astype(jnp.bfloat16).reshape(ex_dev, seq_len, rank_out)
    projected = jnp.einsum(
        "elo,eli->eoi", out_side, in_side, preferred_element_type=jnp.float32
    ).astype(jnp.bfloat16)
    regrouped = lax.all_to_all(projected, ("blk", "sub"), split_axis=1, concat_axis=0, tiled=True)
    held = regrouped.shape[0]
    coords = regrouped.reshape(held, -1, BS)
    every_coord = lax.all_gather(coords, "red", axis=0, tiled=True)
    total_ex, held_blocks = every_coord.shape[:2]
    by_block = every_coord.transpose(1, 0, 2)
    rows = by_block.reshape(held_blocks * total_ex, BS)
    own = jnp.arange(held_blocks * total_ex) // total_ex
    member = own[:, None] == own[None, :]
    gram = jnp.dot(rows, rows.T, preferred_element_type=jnp.float32)
    gram = jnp.where(member, gram, 0.0) / total_ex
    inverse = block_inverse(gram, member, held_blocks)
    query_coords = queries.reshape(queries.shape[0], -1, BS)
    raw = jnp.einsum("qkd,ked->qke", query_coords, by_block, preferred_element_type=jnp.float32)
    raw = raw.reshape(raw.shape[0], -1)
    fold = jnp.sum(inverse.reshape(-1, held_blocks, total_ex), axis=1)
    partial_scores = jnp.dot(raw, fold, precision=HIGH)
    every_score = lax.all_gather(partial_scores, "red", axis=0, tiled=True)
    scores = lax.psum_scatter(every_score, ("blk", "sub"), scatter_dimension=0, tiled=True)
    here = lax.axis_index("red") * held
    scores = lax.dynamic_slice_in_dim(scores, here, held, axis=1)
    return scores * (1.0 / math.sqrt(BLOCKS))


UP, DOWN, ACROSS, OVER, CORE = range(5)


def fused(nz, split, a_hbm, g_hbm, len_ref, pin_hbm, pout_hbm, q_hbm, out_ref, pbuf, abuf, gbuf, qbuf, qt, acc,
          pieces, coords, parts, rbuf, lsem, ssem, rsem, asem_s, asem_r, xsem_s, xsem_r, fsem_s, fsem_r):
    y, z, x, c = (lax.axis_index(name) for name in ("groups", "blk", "red", "sub"))
    rows, rank = pbuf.shape[2:]
    n_tok = abuf.shape[0]
    n_chunk = nz * 2
    me = z * 2 + c

    def slot(zz, xx, cc):
        return (zz * 2 + xx) * 2 + cc

    def remote(src, dst, send, recv, **device):
        return pltpu.make_async_remote_copy(
            src_ref=src, dst_ref=dst, send_sem=send, recv_sem=recv,
            device_id=device, device_id_type=pl.DeviceIdType.MESH)

    own = slot(z, x, c)
    local = [
        pltpu.make_async_copy(pin_hbm, pbuf.at[own, 0], lsem.at[0]),
        pltpu.make_async_copy(pout_hbm, pbuf.at[own, 1], lsem.at[1]),
        pltpu.make_async_copy(q_hbm, qbuf, lsem.at[2]),
        pltpu.make_async_copy(a_hbm, abuf, lsem.at[3]),
        pltpu.make_async_copy(g_hbm, gbuf, lsem.at[4]),
    ]
    for item in local:
        item.start()

    barrier = pltpu.get_barrier_semaphore()

    def greet(**device):
        pl.semaphore_signal(barrier, inc=1, device_id=device, device_id_type=pl.DeviceIdType.MESH)

    pl.when(z < nz - 1)(lambda: greet(blk=lax.min(z + 1, nz - 1)))
    pl.when(z > 0)(lambda: greet(blk=lax.max(z - 1, 0)))
    greet(red=1 - x)
    greet(groups=1 - y)
    greet(sub=1 - c)
    pl.semaphore_wait(barrier, 3 + (z < nz - 1).astype(jnp.int32) + (z > 0).astype(jnp.int32))

    pending = []

    def part(p, at):
        if isinstance(p, int):
            return pbuf.at[at, :, pl.ds(split, rows - split), :]
        return pbuf.at[at, p, pl.ds(0, split), :]

    targets = {UP: lambda: {"blk": lax.min(z + 1, nz - 1)}, DOWN: lambda: {"blk": lax.max(z - 1, 0)},
               ACROSS: lambda: {"red": 1 - x}, OVER: lambda: {"groups": 1 - y}, CORE: lambda: {"sub": 1 - c}}

    def moved(way, p, at):
        return remote(part(p, at), part(p, at), ssem.at[way, p, at], rsem.at[p, at], **targets[way]())

    def send(way, p, at, when=None):
        if when is None:
            moved(way, p, at).start()
        else:
            pl.when(when)(lambda: moved(way, p, at).start())
        pending.append((way, p, at, when))

    def arrived(p, at):
        moved(CORE, p, at).wait_recv()

    def multiply(at, first=False):
        columns = pl.ds(pl.multiple_of(at * rows, rows), rows)
        for side, tokens in enumerate((abuf, gbuf)):
            term = jnp.dot(tokens[:, columns], pbuf[at, side], preferred_element_type=jnp.float32)
            acc[side] = term if first else acc[side] + term

    turns = [sorted(range(nz), key=lambda other: (abs(other - here), other)) for here in range(nz)]

    def turn(k):
        return sum(jnp.where(z == here, turns[here][k], 0) for here in range(nz)).astype(jnp.int32)

    local[0].wait()
    local[1].wait()
    for p in (y, 2):
        send(UP, p, own, z < nz - 1)
        send(DOWN, p, own, z > 0)
        send(ACROSS, p, own)
    for p in (y, 1 - y, 2):
        send(CORE, p, own)

    local[2].wait()
    hh, kb = qt.shape[0], qt.shape[1]
    step_q = 16

    def regroup(i, carry):
        at = pl.ds(pl.multiple_of(i * step_q, step_q), step_q)
        block = jnp.swapaxes(qbuf[at].astype(jnp.float32), 0, 1).astype(jnp.bfloat16)
        block = block.reshape(kb, hh, step_q, rank)
        for h in range(hh):
            qt[h, :, at, :] = block[:, h]
        return carry

    lax.fori_loop(0, qbuf.shape[0] // step_q, regroup, 0)
    local[3].wait()
    local[4].wait()
    multiply(own, True)

    waiting, twin = [], [slot(z, x, 1 - c)]
    for k in range(1, nz + 2):
        fresh = []
        if k < nz:
            zk = turn(k)
            at = slot(zk, x, c)
            for p in (y, 2):
                arrived(p, at)
                send(UP, p, at, jnp.logical_and(zk < z, z < nz - 1))
                send(DOWN, p, at, jnp.logical_and(zk > z, z > 0))
                send(ACROSS, p, at)
                if not isinstance(p, int):
                    send(OVER, p, at)
                send(CORE, p, at)
            fresh.append((zk, x))
        if k <= nz:
            zk = turn(k - 1)
            at = slot(zk, 1 - x, c)
            for p in (y, 2):
                arrived(p, at)
                if not isinstance(p, int):
                    send(OVER, p, at)
                send(CORE, p, at)
            fresh.append((zk, 1 - x))
        for zk, xk in waiting:
            at = slot(zk, xk, c)
            arrived(1 - y, at)
            send(CORE, 1 - y, at)
        for at in twin:
            for p in (y, 1 - y, 2):
                arrived(p, at)
            multiply(at)
        for zk, xk in waiting:
            multiply(slot(zk, xk, c))
        twin = [slot(zk, xk, 1 - c) for zk, xk in waiting]
        waiting = fresh
    for at in twin:
        for p in (y, 1 - y, 2):
            arrived(p, at)
        multiply(at)

    chunk_rows = hh * kb
    old = lax.broadcasted_iota(jnp.int32, (rank, rank), 0)
    new = lax.broadcasted_iota(jnp.int32, (rank, rank), 1)
    inside = jnp.bitwise_and(new, chunk_rows - 1)
    source = new - inside + jnp.bitwise_and(inside, kb - 1) * hh + lax.shift_right_logical(inside, kb.bit_length() - 1)
    order = jnp.where(old == source, 1.0, 0.0).astype(jnp.bfloat16)
    in_side = acc[0].astype(jnp.bfloat16)
    live = lax.broadcasted_iota(jnp.int32, (n_tok, rank), 0) < len_ref[0, 0]
    out_side = jnp.where(live, acc[1], 0.0).astype(jnp.bfloat16)
    out_side = jnp.dot(out_side, order, preferred_element_type=jnp.float32).astype(jnp.bfloat16)
    projected = lax.dot_general(out_side, in_side, (((0,), (0,)), ((), ())), preferred_element_type=jnp.float32)
    pieces[...] = projected.astype(jnp.bfloat16).reshape(pieces.shape)

    def chunk_out(to):
        return remote(pieces.at[to], coords.at[x * n_chunk + me], asem_s.at[to], asem_r.at[me], blk=to // 2, sub=lax.rem(to, 2))

    def chunk_over(to):
        return remote(pieces.at[to], coords.at[x * n_chunk + me], xsem_s.at[to], xsem_r.at[me],
                      blk=to // 2, red=1 - x, sub=lax.rem(to, 2))

    def chunk_in(frm):
        return remote(pieces.at[frm], coords.at[x * n_chunk + frm], asem_s.at[frm], asem_r.at[frm], sub=1 - c)

    def over_in(frm):
        return remote(pieces.at[frm], coords.at[(1 - x) * n_chunk + frm], xsem_s.at[frm], xsem_r.at[frm], red=1 - x)

    middle = n_chunk // 2
    for step in [middle] + [n for away in range(middle - 1, 0, -1) for n in (middle + away, middle - away)][::-1]:
        to = lax.rem(me + step, n_chunk)
        chunk_over(to).start()
        chunk_out(to).start()
    chunk_over(me).start()
    coords[x * n_chunk + me] = pieces[me]
    for step in range(1, n_chunk):
        chunk_in(lax.rem(me + step, n_chunk)).wait_recv()
    for frm in range(n_chunk):
        over_in(frm).wait_recv()

    n_ex = coords.shape[0]
    size = n_ex * kb
    halves = [coords[:, h].reshape(size, rank) for h in range(hh)]
    row = lax.broadcasted_iota(jnp.int32, (size, size), 0)
    col = lax.broadcasted_iota(jnp.int32, (size, size), 1)
    member = jnp.bitwise_and(row, kb - 1) == jnp.bitwise_and(col, kb - 1)
    contract = (((1,), (1,)), ((), ()))
    gram = sum(lax.dot_general(half, half, contract, preferred_element_type=jnp.float32) for half in halves)
    gram = jnp.where(member, gram, 0.0) / n_ex
    ident = jnp.where(row == col, 1.0, 0.0)
    trace = jnp.sum(gram * ident, axis=1, keepdims=True)
    square = jnp.sum(gram * gram, axis=1, keepdims=True)
    trace = jnp.sum(jnp.where(member, trace, 0.0), axis=0, keepdims=True)
    square = jnp.sum(jnp.where(member, square, 0.0), axis=0, keepdims=True)
    damping = DAMPING * trace / BS
    hessian = gram + damping * ident
    scale = lax.rsqrt(square + 2.0 * damping * trace + BS * damping * damping)
    inverse = scale * (2.0 * ident - scale * hessian)

    n_q = qt.shape[2]
    lane = jnp.bitwise_and(lax.broadcasted_iota(jnp.int32, (n_q, size), 1), kb - 1)
    flipped = [half.T for half in halves]
    raw = jnp.zeros((n_q, size), jnp.float32)
    for k in range(kb):
        term = sum(jnp.dot(qt[h, k], flipped[h], preferred_element_type=jnp.float32) for h in range(hh))
        raw = jnp.where(lane == k, term, raw)

    for sweep in range(NS_STEPS):
        image = jnp.dot(hessian, inverse, precision=HIGH, preferred_element_type=jnp.float32)
        rest = 2.0 * ident - image
        if sweep < NS_STEPS - 1:
            inverse = jnp.dot(inverse, rest, precision=HIGH, preferred_element_type=jnp.float32)
    raw = jnp.dot(raw, inverse, precision=HIGH, preferred_element_type=jnp.float32)
    raw = jnp.dot(raw, rest, precision=HIGH, preferred_element_type=jnp.float32)
    ex = lax.broadcasted_iota(jnp.int32, (n_ex, size), 0)
    of_ex = lax.shift_right_logical(lax.broadcasted_iota(jnp.int32, (n_ex, size), 1), kb.bit_length() - 1)
    fold = jnp.where(ex == of_ex, 1.0, 0.0)
    total = lax.dot_general(fold, raw, contract, precision=HIGH, preferred_element_type=jnp.float32)
    parts[...] = total.reshape(parts.shape)

    takers = n_chunk // 2

    def score_out(xx, t):
        to = takers * x + t
        return remote(parts.at[xx], rbuf.at[me], fsem_s.at[xx * takers + t], fsem_r.at[me],
                      blk=to // 2, red=jnp.int32(xx), sub=lax.rem(to, 2))

    def is_self(xx, t):
        return jnp.logical_and(takers * x + t == me, x == xx)

    for xx in range(2):
        for t in range(takers):
            pl.when(jnp.logical_not(is_self(xx, t)))(lambda: score_out(xx, t).start())
    giver = me // takers

    @pl.when(giver == x)
    def _():
        rbuf[me] = parts[x]

    for frm in range(n_chunk):
        landing = remote(parts.at[0], rbuf.at[frm], fsem_s.at[0], fsem_r.at[frm], sub=1 - c)
        pl.when(jnp.logical_not(jnp.logical_and(giver == x, me == frm)))(landing.wait_recv)
    out_ref[...] = jnp.sum(rbuf[...], axis=0)

    for xx in range(2):
        for t in range(takers):
            pl.when(jnp.logical_not(is_self(xx, t)))(lambda: score_out(xx, t).wait_send())
    for step in range(1, n_chunk):
        chunk_out(lax.rem(me + step, n_chunk)).wait_send()
    for to in range(n_chunk):
        chunk_over(to).wait_send()
    for way, p, at, when in pending:
        if when is None:
            moved(way, p, at).wait_send()
        else:
            pl.when(when)(lambda: moved(way, p, at).wait_send())


def on_device_fused(activations, out_grads, lengths, proj_in, proj_out, queries):
    nz = lax.axis_size("blk")
    seq_len, width = activations.shape[2:]
    rows, rank = proj_in.shape
    n_q, held_rows, _ = queries.shape
    hh = BS // rank
    kb = held_rows // hh
    n_chunk = nz * 2
    n_ex = n_chunk * 2
    split = rows * 10 // 16
    anywhere = pl.BlockSpec(memory_space=pltpu.HBM)
    dma = pltpu.SemaphoreType.DMA
    flops = 4 * seq_len * width * rank
    total = pl.pallas_call(
        functools.partial(fused, nz, split),
        out_shape=jax.ShapeDtypeStruct((n_chunk, n_q), jnp.float32),
        in_specs=[anywhere, anywhere, pl.BlockSpec(memory_space=pltpu.SMEM), anywhere, anywhere, anywhere],
        out_specs=pl.BlockSpec(memory_space=pltpu.VMEM),
        scratch_shapes=[
            pltpu.VMEM((n_chunk * 2, 2, rows, rank), jnp.bfloat16),
            pltpu.VMEM((seq_len, width), jnp.bfloat16),
            pltpu.VMEM((seq_len, width), jnp.bfloat16),
            pltpu.VMEM(queries.shape, jnp.bfloat16),
            pltpu.VMEM((hh, kb, n_q, rank), jnp.bfloat16),
            pltpu.VMEM((2, seq_len, rank), jnp.float32),
            pltpu.VMEM((n_chunk, hh, kb, rank), jnp.bfloat16),
            pltpu.VMEM((n_ex, hh, kb, rank), jnp.bfloat16),
            pltpu.VMEM((2, n_chunk, n_q), jnp.float32),
            pltpu.VMEM((n_chunk, n_chunk, n_q), jnp.float32),
            dma((5,)),
            dma((5, 3, n_chunk * 2)),
            dma((3, n_chunk * 2)),
            dma((n_chunk,)),
            dma((n_chunk,)),
            dma((n_chunk,)),
            dma((n_chunk,)),
            dma((n_chunk,)),
            dma((n_chunk,)),
        ],
        compiler_params=pltpu.CompilerParams(collective_id=0, has_side_effects=True, vmem_limit_bytes=63 * 2**20),
        cost_estimate=pl.CostEstimate(flops=flops, bytes_accessed=7 * 2**20, transcendentals=0),
    )(activations.reshape(seq_len, width), out_grads.reshape(seq_len, width), lengths, proj_in, proj_out, queries)
    n_out = n_q * 2 // n_chunk
    me = lax.axis_index("blk") * 2 + lax.axis_index("sub")
    mine = lax.dynamic_slice_in_dim(total, lax.rem(me, n_chunk // 2) * n_out, n_out, axis=1)
    return mine.T * (1.0 / math.sqrt(BLOCKS))


def fits(mesh):
    shape = mesh.shape
    return shape["groups"] == 2 and shape["red"] == 2 and shape["sub"] == 2 and shape["blk"] == 4


def solution(mesh):
    placed = (
        P("red", ("groups", "blk", "sub"), None, None),
        P("red", ("groups", "blk", "sub"), None, None),
        P("red", ("groups", "blk", "sub")),
        P(("blk", "red", "sub"), None),
        P(("blk", "red", "sub"), None),
        P(("groups", "red"), ("blk", "sub"), None),
    )
    return jax.shard_map(
        on_device_fused if fits(mesh) else on_device,
        mesh=mesh,
        in_specs=placed,
        out_specs=P(("groups", "blk", "sub"), "red"),
        check_vma=False,
    )
```
